32 devices in a mesh: grp: 4 (over x, core), dev: 8 (over z, y).
Axes of the slice: x: 2, y: 2, z: 4, core: 2. Of those that a mesh axis runs over, the one named last changes fastest.
Arguments:
- transition: float32 [64, 256, 256], P(('grp', 'dev')), as said below
- observe: float32 [64, 64, 256], P(('grp', 'dev')), may hold values from -0.375 to 0.375
- noise_obs: float32 [64, 64], P(('grp', 'dev')), may hold values from 100 to 1000
- measured: float32 [64, 64], P(('grp', 'dev')), may hold values from -60 to 60
- noise_state: float32 [256, 256], replicated, as said below
- prior_mean: float32 [256], replicated, may hold values from -6 to 6
- prior_cov: float32 [256, 256], replicated, as said below
Outputs:
- means: float32 [64, 256], P(('grp', 'dev'))
- covs: float32 [64, 256, 256], P(('grp', 'dev'))
The draws below stay inside these ranges and needn't reach their ends.
Inputs may be any that keep to these rules, and one draw needn't show every extreme that they name: `transition`: each matrix is (I + G) / sqrt(1.0625) with G of independent entries of deviation 0.25 / sqrt(256). `noise_state`: symmetric positive definite, 0.001 (I + E) with E symmetric of spectral norm well under one. `prior_cov`: symmetric positive definite, I + E with E symmetric of spectral norm well under one.
All inputs are finite; a program needn't handle non-finite values.
Results may differ from the reference program's by a relative error of at most 0.0003.
Values sent between devices are 32-bit elements; how exact they have to be, the bound alone decides.
A program may use at most 128 MiB of HBM per device.

```python
import math
import jax
import jax.numpy as jnp
from jax import lax

NS = 256
NO = 64
STEPS = 64


def draw_transition(key, part):
    noise = jax.random.normal(key, (STEPS, NS, NS), jnp.float32) * (0.25 / jnp.sqrt(jnp.float32(NS)))
    return (jnp.eye(NS, dtype=jnp.float32)[None] + noise) / jnp.sqrt(jnp.float32(1.0625))


def symmetric_part(key):
    base = jax.random.normal(key, (NS, NS), jnp.float32) / jnp.sqrt(jnp.float32(NS))
    return 0.3 * (base + base.T) / jnp.sqrt(jnp.float32(2.0))


def draw_noise_state(key, part):
    return 0.001 * (jnp.eye(NS, dtype=jnp.float32) + symmetric_part(jax.random.fold_in(key, 11)))


def draw_prior_cov(key, part):
    return jnp.eye(NS, dtype=jnp.float32) + symmetric_part(jax.random.fold_in(key, 23))


def shard_levels(stream_key, shape, pieces, least, largest):
    def one(axis_at, shards_of):
        steps = jax.random.uniform(jax.random.fold_in(jax.random.fold_in(stream_key, 6), axis_at), (shards_of,), jnp.float32, least / len(pieces), largest / len(pieces))
        return jnp.repeat(jnp.exp(steps), shape[axis_at] // shards_of).reshape((-1,) + (1,) * (len(shape) - axis_at - 1))

    factor_of = one(*pieces[0])
    for cut in pieces[1:]:
        factor_of = factor_of * one(*cut)
    return factor_of


def centred(key, dims, spread, bound, split=(), kind=jnp.bfloat16):
    drawn = spread * jax.random.normal(key, dims, jnp.float32)
    if split:
        drawn = drawn * shard_levels(key, dims, split, -0.22, 0.18)
    return jnp.clip(drawn, -bound, bound).astype(kind)


def setup_inputs(seed: int = 0) -> dict:
    streams_of = jax.random.split(jax.random.key(seed), 8)
    transition = draw_transition(jax.random.fold_in(streams_of[7], 71), 0)
    observe = centred(streams_of[1], (STEPS, NO, NS), NS ** -0.5, 0.375, ((0, 32),), jnp.float32)
    noise_obs = jnp.clip(jnp.exp(math.log(1000.0) - 2.3025851 * jax.random.uniform(streams_of[2], (STEPS, NO), jnp.float32) ** shard_levels(streams_of[2], (STEPS, NO), ((0, 32),), -0.2, 0.2)), 100.0, 1000.0)
    measured = centred(streams_of[3], (STEPS, NO), 10.0, 60.0, ((0, 32),), jnp.float32)
    noise_state = draw_noise_state(jax.random.fold_in(streams_of[7], 71), 0)
    prior_mean = centred(streams_of[5], (NS,), 1.0, 6.0, (), jnp.float32)
    prior_cov = draw_prior_cov(jax.random.fold_in(streams_of[7], 71), 0)
    return {"transition": transition, "observe": observe, "noise_obs": noise_obs, "measured": measured, "noise_state": noise_state, "prior_mean": prior_mean, "prior_cov": prior_cov}


def reference(transition, observe, noise_obs, measured, noise_state, prior_mean, prior_cov):
    high = lax.Precision.HIGHEST

    def advance(carry, item):
        mean, cov = carry
        forward, sensor, variance, value = item
        mean = jnp.dot(forward, mean, precision=high)
        cov = jnp.dot(jnp.dot(forward, cov, precision=high), forward.T, precision=high) + noise_state
        sensed = jnp.dot(sensor, cov, precision=high)
        innovation = jnp.dot(sensed, sensor.T, precision=high) + jnp.diag(variance)
        gain_rows = jnp.linalg.solve(innovation, sensed)
        mean = mean + jnp.dot(gain_rows.T, value - jnp.dot(sensor, mean, precision=high), precision=high)
        cov = cov - jnp.dot(sensed.T, gain_rows, precision=high)
        return ((mean, cov), (mean, cov))
    _, (means, covs) = lax.scan(advance, (prior_mean, prior_cov), (transition, observe, noise_obs, measured))
    return (means, covs)
```

```python
import functools

import jax
import jax.numpy as jnp
from jax import lax
from jax.experimental import pallas as pl
from jax.experimental.pallas import tpu as pltpu
from jax.sharding import PartitionSpec as P

F32 = jnp.float32
BF16 = jnp.bfloat16
NN = (((1,), (0,)), ((), ()))
NT = (((1,), (1,)), ((), ()))
TN = (((0,), (0,)), ((), ()))
LIMIT = 48 * 1024 * 1024


def one(a, b, dims=NN):
    return lax.dot_general(a, b, dims, preferred_element_type=F32)


def split(a):
    high = a.astype(BF16)
    return high, (a - high.astype(F32)).astype(BF16)


def mm(a, b, dims=NN):
    ah, al = a if isinstance(a, tuple) else split(a)
    bh, bl = b if isinstance(b, tuple) else split(b)
    return one(ah, bh, dims) + (one(ah, bl, dims) + one(al, bh, dims))


def eye(n):
    return (
        lax.broadcasted_iota(jnp.int32, (n, n), 0)
        == lax.broadcasted_iota(jnp.int32, (n, n), 1)
    ).astype(F32)


def resolvent(spread, info):
    n = spread.shape[0]
    coupled = mm(spread, info)
    size = jnp.abs(coupled)
    bound = jnp.minimum(
        jnp.max(jnp.sum(size, axis=0, keepdims=True)),
        jnp.max(jnp.sum(size, axis=1, keepdims=True)),
    )
    unit = eye(n)
    parts = split(coupled)
    scale = 2.0 / (2.0 + bound)
    gap = bound / (2.0 + bound)
    grow = 2.0 / (2.0 - gap * gap)
    guess = (grow * scale) * ((2.0 - scale) * unit - scale * coupled)
    gap = 0.5 * gap * gap * grow

    def go(state):
        sweep, gap, _ = state
        return jnp.logical_and(gap > 2e-6, sweep < 40)

    def sweep(state):
        count, gap, guess = state
        halves = split(guess)
        residue = (unit - guess) - mm(parts, halves)
        grow = 2.0 / (2.0 - gap * gap)
        rh, rl = split(residue)
        change = one(halves[0], rh) + (one(halves[0], rl) + one(halves[1], rh))
        return count + 1, 0.5 * gap * gap * grow, grow * (guess + change)

    return lax.while_loop(go, sweep, (jnp.int32(0), gap, guess))[2]


def read(ref):
    n = ref.shape[1]
    return (
        ref[0:n, :],
        ref[n : 2 * n, :],
        ref[2 * n : 3 * n, :],
        ref[3 * n : 3 * n + 1, :],
        ref[3 * n + 1 : 3 * n + 2, :],
    )


def write(ref, element):
    n = ref.shape[1]
    move, info, spread, off, vec = element
    ref[0:n, :] = move
    ref[n : 2 * n, :] = info
    ref[2 * n : 3 * n, :] = spread
    ref[3 * n : 3 * n + 1, :] = off
    ref[3 * n + 1 : 3 * n + 2, :] = vec
    ref[3 * n + 2 :, :] = jnp.zeros((ref.shape[0] - 3 * n - 2, n), F32)


def wide(row):
    return jnp.broadcast_to(row, (8, row.shape[1]))


def row_mm(row, matrix, dims=NN):
    return mm(wide(row), matrix, dims)[0:1, :]


def combine(first, second):
    move_a, info_a, spr_a, off_a, vec_a = first
    move_b, info_b, spr_b, off_b, vec_b = second
    settle = split(resolvent(spr_a, info_b))
    move_as, spr_as, info_bs, move_bs = split(move_a), split(spr_a), split(info_b), split(move_b)
    seen = split(mm(info_bs, move_as))
    kept = split(mm(settle, move_as))
    narrowed = split(mm(settle, spr_as))
    moved = mm(move_bs, kept)
    spread = mm(mm(move_bs, narrowed), move_bs, NT) + spr_b
    info = mm(kept, seen, TN) + info_a
    shift = row_mm(off_a + row_mm(vec_b, spr_as), settle, NT)
    off = row_mm(shift, move_bs, NT) + off_b
    vec = row_mm(vec_b - row_mm(off_a, info_bs), kept) + vec_a
    return moved, info, spread, off, vec


def apply(state, second):
    spr_a, off_a = state
    move_b, info_b, spr_b, off_b, vec_b = second
    settle = split(resolvent(spr_a, info_b))
    spr_as, move_bs = split(spr_a), split(move_b)
    narrowed = split(mm(settle, spr_as))
    spread = mm(mm(move_bs, narrowed), move_bs, NT) + spr_b
    shift = row_mm(off_a + row_mm(vec_b, spr_as), settle, NT)
    off = row_mm(shift, move_bs, NT) + off_b
    return spread, off


def local_kernel(flag, forward, observe, noise, measured, noise_state, mean, cov, prefixes):
    steps, n = forward.shape[0], forward.shape[1]

    def step(t):
        sensor = observe[t]
        weight = 1.0 / noise[t : t + 1, :]
        weighted = jnp.transpose(sensor) * weight
        info_obs = mm(weighted, sensor)
        vec_obs = row_mm(measured[t : t + 1, :] * weight, sensor)
        process = split(noise_state[...])
        settle = split(resolvent(noise_state[...], info_obs))
        ahead = split(forward[t])
        moved = mm(settle, ahead)
        moveds = split(moved)
        spread = mm(settle, process)
        off = row_mm(row_mm(vec_obs, process), settle, NT)
        info = mm(moveds, split(mm(info_obs, ahead)), TN)
        vec = row_mm(vec_obs, moveds)
        return moved, info, spread, off, vec

    write(prefixes.at[0], step(0))

    @pl.when(flag[0] == 1)
    def _():
        spread, off = apply((cov[...], mean[...]), read(prefixes.at[0]))
        zero = jnp.zeros((n, n), F32)
        write(prefixes.at[0], (zero, zero, spread, off, jnp.zeros((1, n), F32)))

    for t in range(1, steps):
        write(prefixes.at[t], combine(read(prefixes.at[t - 1]), step(t)))


def first_kernel(flag, mine, other, total):
    @pl.when(flag[0] == 1)
    def _():
        write(total, combine(read(other), read(mine)))

    @pl.when(flag[0] == 0)
    def _():
        write(total, combine(read(mine), read(other)))


def round_kernel(flag, mine, before, other, total, entering):
    @pl.when(flag[0] == 1)
    def _():
        write(total, combine(read(other), read(mine)))
        write(entering, combine(read(other), read(before)))

    @pl.when(flag[0] == 0)
    def _():
        write(total, combine(read(mine), read(other)))
        entering[...] = before[...]


def last_kernel(flag, before, other, prefixes, means, covs, spread, off):
    n = before.shape[1]
    spread[...] = before[2 * n : 3 * n, :]
    off[...] = before[3 * n : 3 * n + 1, :]

    @pl.when(flag[0] == 1)
    def _():
        new = apply((other[0:n, :], other[n : n + 1, :]), read(before))
        spread[...] = new[0]
        off[...] = new[1]

    for t in range(prefixes.shape[0]):
        cov, mean = apply((spread[...], off[...]), read(prefixes.at[t]))
        covs[t] = cov
        means[t : t + 1, :] = mean


def call(kernel, args, outs, scratch=()):
    vmem = pl.BlockSpec(memory_space=pltpu.VMEM)
    specs = [pl.BlockSpec(memory_space=pltpu.SMEM)] + [vmem] * (len(args) - 1)
    shapes = [jax.ShapeDtypeStruct(s, F32) for s in outs]
    return pl.pallas_call(
        kernel,
        out_shape=shapes,
        in_specs=specs,
        out_specs=[vmem] * len(outs),
        scratch_shapes=list(scratch),
        compiler_params=pltpu.CompilerParams(vmem_limit_bytes=LIMIT),
    )(*args)


def on_device(transition, observe, noise_obs, measured, noise_state, prior_mean, prior_cov):
    steps, n = transition.shape[0], transition.shape[1]
    packed = 3 * n + 8
    place = {a: lax.axis_index(a) for a in ("dev", "grp")}
    size = {a: lax.axis_size(a) for a in ("dev", "grp")}
    is_first = jnp.logical_and(place["grp"] == 0, place["dev"] == 0)
    (prefixes,) = call(
        local_kernel,
        (
            is_first.astype(jnp.int32)[None],
            transition,
            observe,
            noise_obs,
            measured,
            noise_state,
            prior_mean[None],
            prior_cov,
        ),
        [(steps, packed, n)],
    )
    rounds = [(a, 1 << b) for a in ("dev", "grp") for b in range(size[a].bit_length() - 1)]
    total = prefixes[steps - 1]
    neutral = jnp.concatenate([jnp.eye(n, dtype=F32), jnp.zeros((packed - n, n), F32)])
    before = neutral
    for count, (axis, gap) in enumerate(rounds):
        upper = (place[axis] // gap) % 2
        flag = upper.astype(jnp.int32)[None]
        if count == len(rounds) - 1:
            pairs = [(i, i ^ gap) for i in range(size[axis]) if not i & gap]
            other = lax.ppermute(total[2 * n :], axis, pairs)
            means, covs = call(
                last_kernel,
                (flag, before, other, prefixes),
                [(steps, n), (steps, n, n)],
                [pltpu.VMEM((n, n), F32), pltpu.VMEM((1, n), F32)],
            )
        else:
            other = lax.ppermute(total, axis, [(i, i ^ gap) for i in range(size[axis])])
            if count == 0:
                (total,) = call(first_kernel, (flag, total, other), [(packed, n)])
                before = jnp.where(upper == 1, other, neutral)
            else:
                total, before = call(
                    round_kernel, (flag, total, before, other), [(packed, n)] * 2
                )
    return means, covs


def solution(mesh):
    both = ("grp", "dev")
    return jax.shard_map(
        on_device,
        mesh=mesh,
        in_specs=(P(both, None, None), P(both, None, None), P(both, None), P(both, None), P(), P(), P()),
        out_specs=(P(both, None), P(both, None, None)),
        check_vma=False,
    )
```

```python
import functools

import jax
import jax.numpy as jnp
from jax import lax
from jax.experimental import pallas as pl
from jax.experimental.pallas import tpu as pltpu
from jax.sharding import PartitionSpec as P

F32 = jnp.float32
BF16 = jnp.bfloat16
NN = (((1,), (0,)), ((), ()))
NT = (((1,), (1,)), ((), ()))
TN = (((0,), (0,)), ((), ()))
LIMIT = 48 * 1024 * 1024


def one(a, b, dims=NN):
    return lax.dot_general(a, b, dims, preferred_element_type=F32)


def split(a):
    high = a.astype(BF16)
    return high, (a - high.astype(F32)).astype(BF16)


def mm(a, b, dims=NN):
    ah, al = a if isinstance(a, tuple) else split(a)
    bh, bl = b if isinstance(b, tuple) else split(b)
    return one(ah, bh, dims) + (one(ah, bl, dims) + one(al, bh, dims))


def eye(n):
    return (
        lax.broadcasted_iota(jnp.int32, (n, n), 0)
        == lax.broadcasted_iota(jnp.int32, (n, n), 1)
    ).astype(F32)


def resolvent(spread, info):
    n = spread.shape[0]
    coupled = mm(spread, info)
    size = jnp.abs(coupled)
    bound = jnp.minimum(
        jnp.max(jnp.sum(size, axis=0, keepdims=True)),
        jnp.max(jnp.sum(size, axis=1, keepdims=True)),
    )
    unit = eye(n)
    parts = split(coupled)
    scale = 2.0 / (2.0 + bound)
    gap = bound / (2.0 + bound)
    grow = 2.0 / (2.0 - gap * gap)
    guess = (grow * scale) * ((2.0 - scale) * unit - scale * coupled)
    gap = 0.5 * gap * gap * grow

    def go(state):
        sweep, gap, _ = state
        return jnp.logical_and(gap > 1e-5, sweep < 40)

    def sweep(state):
        count, gap, guess = state
        halves = split(guess)
        residue = (unit - guess) - mm(parts, halves)
        grow = 2.0 / (2.0 - gap * gap)
        change = one(halves[0], residue.astype(BF16))
        return count + 1, 0.5 * gap * gap * grow, grow * (guess + change)

    return lax.while_loop(go, sweep, (jnp.int32(0), gap, guess))[2]


def packed_rows(n):
    return 2 * n + n // 2 + 8


def join(top, corner):
    h = top.shape[0]
    return jnp.concatenate(
        [top, jnp.concatenate([jnp.transpose(top[:, h:]), corner], axis=1)], axis=0
    )


def read_state(ref, at=0):
    n = ref.shape[1]
    h = n // 2
    spread = join(ref[at : at + h, :], ref[at + h : at + n, 0:h])
    return spread, ref[at + n : at + n + 1, :]


def read(ref):
    n = ref.shape[1]
    h = n // 2
    spread, off = read_state(ref, n + h)
    info = join(ref[n : n + h, :], ref[n + 2 * h : n + 3 * h, h:])
    return ref[0:n, :], info, spread, off, ref[n + 3 * h + 1 : n + 3 * h + 2, :]


def write_state(ref, state, at=0, corner=None, vec=None):
    n = ref.shape[1]
    h = n // 2
    spread, off = state
    ref[at : at + h, :] = spread[0:h, :]
    ref[at + h : at + n, 0:h] = spread[h:, h:]
    ref[at + h : at + n, h:] = jnp.zeros((h, h), F32) if corner is None else corner
    ref[at + n : at + n + 8, :] = jnp.zeros((8, n), F32)
    ref[at + n : at + n + 1, :] = off
    if vec is not None:
        ref[at + n + 1 : at + n + 2, :] = vec


def write(ref, element):
    n = ref.shape[1]
    h = n // 2
    move, info, spread, off, vec = element
    ref[0:n, :] = move
    ref[n : n + h, :] = info[0:h, :]
    write_state(ref, (spread, off), n + h, info[h:, h:], vec)


def wide(row):
    return jnp.broadcast_to(row, (8, row.shape[1]))


def row_mm(row, matrix, dims=NN):
    return mm(wide(row), matrix, dims)[0:1, :]


def combine(first, second):
    move_a, info_a, spr_a, off_a, vec_a = first
    move_b, info_b, spr_b, off_b, vec_b = second
    settle = split(resolvent(spr_a, info_b))
    move_as, spr_as, info_bs, move_bs = split(move_a), split(spr_a), split(info_b), split(move_b)
    seen = split(mm(info_bs, move_as))
    kept = split(mm(settle, move_as))
    narrowed = split(mm(settle, spr_as))
    moved = mm(move_bs, kept)
    spread = mm(mm(move_bs, narrowed), move_bs, NT) + spr_b
    info = mm(kept, seen, TN) + info_a
    shift = row_mm(off_a + row_mm(vec_b, spr_as), settle, NT)
    off = row_mm(shift, move_bs, NT) + off_b
    vec = row_mm(vec_b - row_mm(off_a, info_bs), kept) + vec_a
    return moved, info, spread, off, vec


def apply(state, second):
    spr_a, off_a = state
    move_b, info_b, spr_b, off_b, vec_b = second
    settle = split(resolvent(spr_a, info_b))
    spr_as, move_bs = split(spr_a), split(move_b)
    narrowed = split(mm(settle, spr_as))
    spread = mm(mm(move_bs, narrowed), move_bs, NT) + spr_b
    shift = row_mm(off_a + row_mm(vec_b, spr_as), settle, NT)
    off = row_mm(shift, move_bs, NT) + off_b
    return spread, off


def fetch(sources, buffers, sems):
    copies = []
    for source, buffer in zip(sources, buffers):
        copies.append(pltpu.make_async_copy(source, buffer, sems.at[len(copies)]))
    for copy in copies:
        copy.start()
    for copy in copies:
        copy.wait()


def local_kernel(flag, prefixes, total, forward, observe, noise, measured, noise_state, mean, cov):
    steps, n = forward.shape[0], forward.shape[1]

    def step(t):
        sensor = observe[t]
        weight = 1.0 / noise[t : t + 1, :]
        weighted = jnp.transpose(sensor) * weight
        info_obs = mm(weighted, sensor)
        vec_obs = row_mm(measured[t : t + 1, :] * weight, sensor)
        process = split(noise_state[...])
        settle = split(resolvent(noise_state[...], info_obs))
        ahead = split(forward[t])
        moved = mm(settle, ahead)
        moveds = split(moved)
        spread = mm(settle, process)
        off = row_mm(row_mm(vec_obs, process), settle, NT)
        info = mm(moveds, split(mm(info_obs, ahead)), TN)
        vec = row_mm(vec_obs, moveds)
        return moved, info, spread, off, vec

    write(prefixes.at[0], step(0))

    @pl.when(flag[0] == 1)
    def _():
        state = apply((cov[...], mean[...]), read(prefixes.at[0]))
        zero = jnp.zeros((n, n), F32)
        write(prefixes.at[0], (zero, zero) + state + (jnp.zeros((1, n), F32),))

    for t in range(1, steps):
        write(prefixes.at[t], combine(read(prefixes.at[t - 1]), step(t)))
    total[...] = prefixes[steps - 1]


def pair_kernel(flag, total, mine, other):
    @pl.when(flag[0] == 1)
    def _():
        write(total, combine(read(other), read(mine)))

    @pl.when(flag[0] == 0)
    def _():
        write(total, combine(read(mine), read(other)))


def round_kernel(flag, total, entering, mine, other, before=None):
    n = mine.shape[1]

    @pl.when(flag[0] == 1)
    def _():
        write(total, combine(read(other), read(mine)))
        if before is None:
            entering[...] = other[...]
        else:
            write(entering, combine(read(other), read(before)))

    @pl.when(flag[0] == 0)
    def _():
        write(total, combine(read(mine), read(other)))
        if before is None:
            zero, row = jnp.zeros((n, n), F32), jnp.zeros((1, n), F32)
            write(entering, (eye(n), zero, zero, row, row))
        else:
            entering[...] = before[...]


def last_kernel(flag, own, sent, before, other, mine, partner):
    n = before.shape[1]

    @pl.when(flag[0] == 1)
    def _():
        write_state(own, apply(read_state(other), read(before)))

    @pl.when(flag[0] == 0)
    def _():
        write_state(own, read_state(before, n + n // 2))

    @pl.when(flag[1] == 1)
    def _():
        sent[...] = own[...]
        write_state(own, apply(read_state(sent), read(partner)))

    @pl.when(flag[1] == 0)
    def _():
        write_state(sent, apply(read_state(own), read(mine)))


def final_kernel(flag, means, covs, own, other, prefixes):
    def finish(entering):
        for t in range(prefixes.shape[0]):
            cov, mean = apply(read_state(entering), read(prefixes.at[t]))
            covs[t] = cov
            means[t : t + 1, :] = mean

    @pl.when(flag[0] == 1)
    def _():
        finish(own)

    @pl.when(flag[0] == 0)
    def _():
        finish(other)


def call(kernel, args, outs):
    flag, operands = args[0], args[1:]
    vmem = pl.BlockSpec(memory_space=pltpu.VMEM)

    def body(flag, *refs):
        count, made = len(operands), len(outs)
        sources, results = refs[:count], refs[count : count + made]
        buffers, sems = refs[count + made : -1], refs[-1]
        fetch(sources, buffers, sems)
        kernel(flag, *results, *buffers)

    return pl.pallas_call(
        body,
        out_shape=[jax.ShapeDtypeStruct(s, F32) for s in outs],
        in_specs=[pl.BlockSpec(memory_space=pltpu.SMEM)]
        + [pl.BlockSpec(memory_space=pltpu.HBM)] * len(operands),
        out_specs=[vmem] * len(outs),
        scratch_shapes=[pltpu.VMEM(a.shape, F32) for a in operands]
        + [pltpu.SemaphoreType.DMA((len(operands),))],
        name=kernel.__name__,
        compiler_params=pltpu.CompilerParams(vmem_limit_bytes=LIMIT),
    )(*args)


def on_device(transition, observe, noise_obs, measured, noise_state, prior_mean, prior_cov):
    steps, n = transition.shape[0], transition.shape[1]
    rows = packed_rows(n)
    axes = ("grp", "dev")
    grp, dev = lax.axis_index("grp"), lax.axis_index("dev")
    groups, devs = lax.axis_size("grp"), lax.axis_size("dev")
    places = [(g, d) for g in range(groups) for d in range(devs)]
    carries = (grp + dev) % 2

    def flags(*values):
        return jnp.stack([jnp.asarray(v, jnp.int32) for v in values])

    def send(array, route):
        pairs = []
        for g, d in places:
            to = route(g, d)
            if to is not None:
                pairs.append((g * devs + d, to[0] * devs + to[1]))
        return lax.ppermute(array, axes, pairs)

    first = jnp.logical_and(grp == 0, dev == 0)
    prefixes, mine = call(
        local_kernel,
        (
            flags(first),
            transition,
            observe,
            noise_obs,
            measured,
            noise_state,
            prior_mean[None],
            prior_cov,
        ),
        [(steps, rows, n), (rows, n)],
    )
    partner = send(mine, lambda g, d: None if (g + d) % 2 else (g, d ^ 1))
    odd = dev % 2
    (total,) = call(pair_kernel, (flags(jnp.where(carries == 1, odd, 2)), mine, partner), [(rows, n)])
    rounds = [("dev", 1 << b) for b in range(1, devs.bit_length() - 1)]
    rounds += [("grp", 1 << b) for b in range(groups.bit_length() - 1)]
    before = None
    for count, (axis, gap) in enumerate(rounds):
        upper = ((dev if axis == "dev" else grp) // gap) % 2
        flag = jnp.where(carries == 1, upper, 2)

        def across(g, d):
            if not (g + d) % 2:
                return None
            if axis == "dev":
                return (g, d ^ gap)
            return (g ^ gap, d ^ 1 if gap == 1 else d)

        if count < len(rounds) - 1:
            other = send(total, across)
            total, before = call(
                round_kernel,
                (flags(flag), total, other) + (() if before is None else (before,)),
                [(rows, n)] * 2,
            )
        else:
            other = send(
                total[rows - n - 8 :], lambda g, d: None if g & gap else across(g, d)
            )
            own, sent = call(
                last_kernel,
                (flags(flag, jnp.where(carries == 1, odd, 2)), before, other, mine, partner),
                [(n + 8, n)] * 2,
            )
    received = send(sent, lambda g, d: (g, d ^ 1) if (g + d) % 2 else None)
    means, covs = call(
        final_kernel, (flags(carries), own, received, prefixes), [(steps, n), (steps, n, n)]
    )
    return means, covs


def solution(mesh):
    both = ("grp", "dev")
    return jax.shard_map(
        on_device,
        mesh=mesh,
        in_specs=(P(both, None, None), P(both, None, None), P(both, None), P(both, None), P(), P(), P()),
        out_specs=(P(both, None), P(both, None, None)),
        check_vma=False,
    )
```

```python
import functools

import jax
import jax.numpy as jnp
from jax import lax
from jax.experimental import pallas as pl
from jax.experimental.pallas import tpu as pltpu
from jax.sharding import PartitionSpec as P

F32 = jnp.float32
BF16 = jnp.bfloat16
NN = (((1,), (0,)), ((), ()))
NT = (((1,), (1,)), ((), ()))
TN = (((0,), (0,)), ((), ()))
LIMIT = 32 * 1024 * 1024
WHOLE = 60 * 1024 * 1024


def one(a, b, dims=NN):
    return lax.dot_general(a, b, dims, preferred_element_type=F32)


def split(a):
    high = a.astype(BF16)
    return high, (a - high.astype(F32)).astype(BF16)


def mm(a, b, dims=NN):
    ah, al = a if isinstance(a, tuple) else split(a)
    bh, bl = b if isinstance(b, tuple) else split(b)
    return one(ah, bh, dims) + (one(ah, bl, dims) + one(al, bh, dims))


def eye(n):
    return (
        lax.broadcasted_iota(jnp.int32, (n, n), 0)
        == lax.broadcasted_iota(jnp.int32, (n, n), 1)
    ).astype(F32)


def resolvents(pairs):
    n = pairs[0][0].shape[0]
    coupled = [mm(spread, info) for spread, info in pairs]
    bound = jnp.float32(0.0)
    for matrix in coupled:
        size = jnp.abs(matrix)
        rows = jnp.max(jnp.sum(size, axis=0, keepdims=True))
        columns = jnp.max(jnp.sum(size, axis=1, keepdims=True))
        bound = jnp.maximum(bound, jnp.minimum(rows, columns))
    unit = eye(n)
    parts = [split(matrix) for matrix in coupled]
    scale = 2.0 / (2.0 + bound)
    gap = bound / (2.0 + bound)
    grow = 2.0 / (2.0 - gap * gap)
    guesses = tuple(
        (grow * scale) * ((2.0 - scale) * unit - scale * matrix) for matrix in coupled
    )
    gap = 0.5 * gap * gap * grow

    def go(state):
        sweep, gap, _ = state
        return jnp.logical_and(gap > 1e-5, sweep < 40)

    def sweep(state):
        count, gap, guesses = state
        grow = 2.0 / (2.0 - gap * gap)
        halves = [split(guess) for guess in guesses]
        residues = [
            (unit - guess) - mm(part, half)
            for guess, part, half in zip(guesses, parts, halves)
        ]
        guesses = tuple(
            grow * (guess + one(half[0], residue.astype(BF16)))
            for guess, half, residue in zip(guesses, halves, residues)
        )
        return count + 1, 0.5 * gap * gap * grow, guesses

    return lax.while_loop(go, sweep, (jnp.int32(0), gap, guesses))[2]


def resolvent(spread, info):
    return resolvents([(spread, info)])[0]


def packed_rows(n):
    return 2 * n + n // 2 + 8


def join(top, corner):
    h = top.shape[0]
    return jnp.concatenate(
        [top, jnp.concatenate([jnp.transpose(top[:, h:]), corner], axis=1)], axis=0
    )


def read_state(ref, at=0):
    n = ref.shape[1]
    h = n // 2
    spread = join(ref[at : at + h, :], ref[at + h : at + n, 0:h])
    return spread, ref[at + n : at + n + 1, :]


def read(ref):
    n = ref.shape[1]
    h = n // 2
    spread, off = read_state(ref, n + h)
    info = join(ref[n : n + h, :], ref[n + 2 * h : n + 3 * h, h:])
    return ref[0:n, :], info, spread, off, ref[n + 3 * h + 1 : n + 3 * h + 2, :]


def write_state(ref, state, at=0, corner=None, vec=None):
    n = ref.shape[1]
    h = n // 2
    spread, off = state
    ref[at : at + h, :] = spread[0:h, :]
    ref[at + h : at + n, 0:h] = spread[h:, h:]
    ref[at + h : at + n, h:] = jnp.zeros((h, h), F32) if corner is None else corner
    ref[at + n : at + n + 8, :] = jnp.zeros((8, n), F32)
    ref[at + n : at + n + 1, :] = off
    if vec is not None:
        ref[at + n + 1 : at + n + 2, :] = vec


def write(ref, element):
    n = ref.shape[1]
    h = n // 2
    move, info, spread, off, vec = element
    ref[0:n, :] = move
    ref[n : n + h, :] = info[0:h, :]
    write_state(ref, (spread, off), n + h, info[h:, h:], vec)


def wide(row):
    return jnp.broadcast_to(row, (8, row.shape[1]))


def row_mm(row, matrix, dims=NN):
    return mm(wide(row), matrix, dims)[0:1, :]


def combines(firsts, seconds):
    settles = resolvents([(first[2], second[1]) for first, second in zip(firsts, seconds)])
    return [combined(*item) for item in zip(firsts, seconds, settles)]


def combine(first, second):
    return combines([first], [second])[0]


def combined(first, second, settle):
    move_a, info_a, spr_a, off_a, vec_a = first
    move_b, info_b, spr_b, off_b, vec_b = second
    settle = split(settle)
    move_as, spr_as, info_bs, move_bs = split(move_a), split(spr_a), split(info_b), split(move_b)
    seen = split(mm(info_bs, move_as))
    kept = split(mm(settle, move_as))
    narrowed = split(mm(settle, spr_as))
    moved = mm(move_bs, kept)
    spread = mm(mm(move_bs, narrowed), move_bs, NT) + spr_b
    info = mm(kept, seen, TN) + info_a
    shift = row_mm(off_a + row_mm(vec_b, spr_as), settle, NT)
    off = row_mm(shift, move_bs, NT) + off_b
    vec = row_mm(vec_b - row_mm(off_a, info_bs), kept) + vec_a
    return moved, info, spread, off, vec


def applies(state, seconds):
    settles = resolvents([(state[0], second[1]) for second in seconds])
    return [applied(state, *item) for item in zip(seconds, settles)]


def apply(state, second):
    return applies(state, [second])[0]


def applied(state, second, settle):
    spr_a, off_a = state
    move_b, info_b, spr_b, off_b, vec_b = second
    settle = split(settle)
    spr_as, move_bs = split(spr_a), split(move_b)
    narrowed = split(mm(settle, spr_as))
    spread = mm(mm(move_bs, narrowed), move_bs, NT) + spr_b
    shift = row_mm(off_a + row_mm(vec_b, spr_as), settle, NT)
    off = row_mm(shift, move_bs, NT) + off_b
    return spread, off


def fetch(sources, buffers, sems):
    copies = []
    for source, buffer in zip(sources, buffers):
        copies.append(pltpu.make_async_copy(source, buffer, sems.at[len(copies)]))
    for copy in copies:
        copy.start()
    for copy in copies:
        copy.wait()


def local_kernel(flag, prefixes, total, forward, observe, noise, measured, noise_state, mean, cov):
    steps, n = forward.shape[0], forward.shape[1]
    process = split(noise_state[...])
    weights = [1.0 / noise[t : t + 1, :] for t in range(steps)]
    infos = [mm(jnp.transpose(observe[t]) * weights[t], observe[t]) for t in range(steps)]
    settles = resolvents([(noise_state[...], info) for info in infos])
    elements = []
    for t in range(steps):
        vec_obs = row_mm(measured[t : t + 1, :] * weights[t], observe[t])
        settle, ahead = split(settles[t]), split(forward[t])
        moved = mm(settle, ahead)
        moveds = split(moved)
        spread = mm(settle, process)
        off = row_mm(row_mm(vec_obs, process), settle, NT)
        info = mm(moveds, split(mm(infos[t], ahead)), TN)
        elements.append((moved, info, spread, off, row_mm(vec_obs, moveds)))

    @pl.when(flag[0] == 1)
    def _():
        zero, row = jnp.zeros((n, n), F32), jnp.zeros((1, n), F32)
        state = (cov[...], mean[...])
        for t in range(steps):
            state = apply(state, elements[t])
            write(prefixes.at[t], (zero, zero) + state + (row,))

    @pl.when(flag[0] == 0)
    def _():
        running = elements[0]
        write(prefixes.at[0], running)
        for t in range(1, steps):
            running = combine(running, elements[t])
            write(prefixes.at[t], running)

    total[...] = prefixes[steps - 1]


def total_kernel(flag, total, mine, other):
    @pl.when(flag[0] == 1)
    def _():
        write(total, combine(read(other), read(mine)))

    @pl.when(flag[0] == 0)
    def _():
        write(total, combine(read(mine), read(other)))


def entering_kernel(flag, entering, other, before=None):
    n = other.shape[1]

    @pl.when(flag[0] == 1)
    def _():
        if before is None:
            entering[...] = other[...]
        else:
            write(entering, combine(read(other), read(before)))

    @pl.when(flag[0] == 0)
    def _():
        if before is None:
            zero, row = jnp.zeros((n, n), F32), jnp.zeros((1, n), F32)
            write(entering, (eye(n), zero, zero, row, row))
        else:
            entering[...] = before[...]


def state_kernel(flag, state, mine, other):
    n = mine.shape[1]

    def go(first, second):
        write_state(state, apply(read_state(first, n + n // 2), read(second)))

    @pl.when(flag[0] == 1)
    def _():
        go(other, mine)

    @pl.when(flag[0] == 0)
    def _():
        go(mine, other)


def compose_kernel(flag, composed, other, before, prefixes):
    steps = range(prefixes.shape[0])

    @pl.when(flag[0] == 1)
    def _():
        write(before, combine(read(other), read(before)))

    made = combines([read(before)] * len(steps), [read(prefixes.at[t]) for t in steps])
    for t in steps:
        write(composed.at[t], made[t])


def final_kernel(flag, means, covs, other, prefixes):
    n = other.shape[1]
    steps = range(prefixes.shape[0])

    @pl.when(flag[0] == 1)
    def _():
        made = applies(read_state(other), [read(prefixes.at[t]) for t in steps])
        for t in steps:
            covs[t] = made[t][0]
            means[t : t + 1, :] = made[t][1]

    @pl.when(flag[0] == 0)
    def _():
        for t in steps:
            cov, mean = read_state(prefixes.at[t], n + n // 2)
            covs[t] = cov
            means[t : t + 1, :] = mean


def call(kernel, args, outs):
    flag, operands = args[0], args[1:]
    vmem = pl.BlockSpec(memory_space=pltpu.VMEM)

    def body(flag, *refs):
        count, made = len(operands), len(outs)
        sources, results = refs[:count], refs[count : count + made]
        buffers, sems = refs[count + made : -1], refs[-1]
        fetch(sources, buffers, sems)
        kernel(flag, *results, *buffers)

    return pl.pallas_call(
        body,
        out_shape=[jax.ShapeDtypeStruct(s, F32) for s in outs],
        in_specs=[pl.BlockSpec(memory_space=pltpu.SMEM)]
        + [pl.BlockSpec(memory_space=pltpu.HBM)] * len(operands),
        out_specs=[vmem] * len(outs),
        scratch_shapes=[pltpu.VMEM(a.shape, F32) for a in operands]
        + [pltpu.SemaphoreType.DMA((len(operands),))],
        name=kernel.__name__,
        cost_estimate=pl.CostEstimate(
            flops=3000000000, bytes_accessed=4000000, transcendentals=0
        ),
        compiler_params=pltpu.CompilerParams(
            vmem_limit_bytes=WHOLE if kernel is local_kernel else LIMIT
        ),
    )(*args)


def on_device(transition, observe, noise_obs, measured, noise_state, prior_mean, prior_cov):
    steps, n = transition.shape[0], transition.shape[1]
    rows = packed_rows(n)
    axes = ("grp", "dev")
    grp, dev = lax.axis_index("grp"), lax.axis_index("dev")
    groups, devs = lax.axis_size("grp"), lax.axis_size("dev")
    places = [(g, d) for g in range(groups) for d in range(devs)]

    def flags(value):
        return jnp.asarray(value, jnp.int32)[None]

    def send(array, route):
        pairs = []
        for g, d in places:
            to = route(g, d)
            if to is not None:
                pairs.append((g * devs + d, to[0] * devs + to[1]))
        return lax.ppermute(array, axes, pairs)

    first = jnp.logical_and(grp == 0, dev == 0)
    prefixes, total = call(
        local_kernel,
        (
            flags(first),
            transition,
            observe,
            noise_obs,
            measured,
            noise_state,
            prior_mean[None],
            prior_cov,
        ),
        [(steps, rows, n), (rows, n)],
    )
    rounds = [("dev", 1 << b) for b in range(devs.bit_length() - 1)]
    rounds += [("grp", 1 << b) for b in range(groups.bit_length() - 1)]
    before = None
    for count, (axis, gap) in enumerate(rounds):
        upper = flags(((dev if axis == "dev" else grp) // gap) % 2)

        def across(g, d):
            return (g, d ^ gap) if axis == "dev" else (g ^ gap, d)

        if count < len(rounds) - 1:
            other = send(total, across)
            if before is not None:
                other, before = lax.optimization_barrier((other, before))
            if count < len(rounds) - 2:
                (total,) = call(total_kernel, (upper, total, other), [(rows, n)])
                (before,) = call(
                    entering_kernel,
                    (upper, other) + (() if before is None else (before,)),
                    [(rows, n)],
                )
            else:
                (state,) = call(state_kernel, (upper, total, other), [(n + 8, n)])
                (composed,) = call(
                    compose_kernel, (upper, other, before, prefixes), [(steps, rows, n)]
                )
        else:
            received = send(state, lambda g, d: None if g & gap else across(g, d))
            means, covs = call(
                final_kernel, (upper, received, composed), [(steps, n), (steps, n, n)]
            )
    return means, covs


def solution(mesh):
    both = ("grp", "dev")
    return jax.shard_map(
        on_device,
        mesh=mesh,
        in_specs=(P(both, None, None), P(both, None, None), P(both, None), P(both, None), P(), P(), P()),
        out_specs=(P(both, None), P(both, None, None)),
        check_vma=False,
    )
```

```python
import functools

import jax
import jax.numpy as jnp
from jax import lax
from jax.experimental import pallas as pl
from jax.experimental.pallas import tpu as pltpu
from jax.sharding import PartitionSpec as P

F32 = jnp.float32
BF16 = jnp.bfloat16
NN = (((1,), (0,)), ((), ()))
NT = (((1,), (1,)), ((), ()))
TN = (((0,), (0,)), ((), ()))
LIMIT = 32 * 1024 * 1024
WHOLE = 60 * 1024 * 1024


def one(a, b, dims=NN):
    return lax.dot_general(a, b, dims, preferred_element_type=F32)


def split(a):
    high = a.astype(BF16)
    return high, (a - high.astype(F32)).astype(BF16)


def mm(a, b, dims=NN):
    ah, al = a if isinstance(a, tuple) else split(a)
    bh, bl = b if isinstance(b, tuple) else split(b)
    return one(ah, bh, dims) + (one(ah, bl, dims) + one(al, bh, dims))


def eye(n):
    return (
        lax.broadcasted_iota(jnp.int32, (n, n), 0)
        == lax.broadcasted_iota(jnp.int32, (n, n), 1)
    ).astype(F32)


def resolvents(pairs):
    n = pairs[0][0].shape[0]
    coupled = [mm(spread, info) for spread, info in pairs]
    bound = jnp.float32(0.0)
    for matrix in coupled:
        size = jnp.abs(matrix)
        rows = jnp.max(jnp.sum(size, axis=0, keepdims=True))
        columns = jnp.max(jnp.sum(size, axis=1, keepdims=True))
        bound = jnp.maximum(bound, jnp.minimum(rows, columns))
    unit = eye(n)
    parts = [split(matrix) for matrix in coupled]
    scale = 2.0 / (2.0 + bound)
    gap = bound / (2.0 + bound)
    grow = 2.0 / (2.0 - gap * gap)
    guesses = tuple(
        (grow * scale) * ((2.0 - scale) * unit - scale * matrix) for matrix in coupled
    )
    gap = 0.5 * gap * gap * grow

    def go(state):
        sweep, gap, _ = state
        return jnp.logical_and(gap > 1e-5, sweep < 40)

    def sweep(state):
        count, gap, guesses = state
        grow = 2.0 / (2.0 - gap * gap)
        halves = [split(guess) for guess in guesses]
        residues = [
            (unit - guess) - mm(part, half)
            for guess, part, half in zip(guesses, parts, halves)
        ]
        guesses = tuple(
            grow * (guess + one(half[0], residue.astype(BF16)))
            for guess, half, residue in zip(guesses, halves, residues)
        )
        return count + 1, 0.5 * gap * gap * grow, guesses

    return lax.while_loop(go, sweep, (jnp.int32(0), gap, guesses))[2]


def resolvent(spread, info):
    return resolvents([(spread, info)])[0]


def packed_rows(n):
    return 2 * n + n // 2 + 8


def join(top, corner):
    h = top.shape[0]
    return jnp.concatenate(
        [top, jnp.concatenate([jnp.transpose(top[:, h:]), corner], axis=1)], axis=0
    )


def read_state(ref, at=0):
    n = ref.shape[1]
    h = n // 2
    spread = join(ref[at : at + h, :], ref[at + h : at + n, 0:h])
    return spread, ref[at + n : at + n + 1, :]


def compact_rows(n):
    return n // 2 + n // 4 + 8


def write_compact(ref, state):
    n = ref.shape[1]
    h, q = n // 2, n // 4
    spread, off = state
    ref[0:h, :] = spread[0:h, :]
    ref[h : h + q, 0:h] = spread[h : h + q, h:]
    ref[h : h + q, h:] = spread[h + q :, h:]
    ref[h + q :, :] = wide(off)


def read_compact(ref):
    n = ref.shape[1]
    h, q = n // 2, n // 4
    corner = jnp.concatenate([ref[h : h + q, 0:h], ref[h : h + q, h:]], axis=0)
    return join(ref[0:h, :], corner), ref[h + q : h + q + 1, :]


def read(ref):
    n = ref.shape[1]
    h = n // 2
    spread, off = read_state(ref, n + h)
    info = join(ref[n : n + h, :], ref[n + 2 * h : n + 3 * h, h:])
    return ref[0:n, :], info, spread, off, ref[n + 3 * h + 1 : n + 3 * h + 2, :]


def write_state(ref, state, at=0, corner=None, vec=None):
    n = ref.shape[1]
    h = n // 2
    spread, off = state
    ref[at : at + h, :] = spread[0:h, :]
    ref[at + h : at + n, 0:h] = spread[h:, h:]
    ref[at + h : at + n, h:] = jnp.zeros((h, h), F32) if corner is None else corner
    ref[at + n : at + n + 8, :] = jnp.zeros((8, n), F32)
    ref[at + n : at + n + 1, :] = off
    if vec is not None:
        ref[at + n + 1 : at + n + 2, :] = vec


def write(ref, element):
    n = ref.shape[1]
    h = n // 2
    move, info, spread, off, vec = element
    ref[0:n, :] = move
    ref[n : n + h, :] = info[0:h, :]
    write_state(ref, (spread, off), n + h, info[h:, h:], vec)


def wide(row):
    return jnp.broadcast_to(row, (8, row.shape[1]))


def row_mm(row, matrix, dims=NN):
    return mm(wide(row), matrix, dims)[0:1, :]


def combines(firsts, seconds):
    settles = resolvents([(first[2], second[1]) for first, second in zip(firsts, seconds)])
    return [combined(*item) for item in zip(firsts, seconds, settles)]


def combine(first, second):
    return combines([first], [second])[0]


def combined(first, second, settle):
    move_a, info_a, spr_a, off_a, vec_a = first
    move_b, info_b, spr_b, off_b, vec_b = second
    settle = split(settle)
    move_as, spr_as, info_bs, move_bs = split(move_a), split(spr_a), split(info_b), split(move_b)
    seen = split(mm(info_bs, move_as))
    kept = split(mm(settle, move_as))
    narrowed = split(mm(settle, spr_as))
    moved = mm(move_bs, kept)
    spread = mm(mm(move_bs, narrowed), move_bs, NT) + spr_b
    info = mm(kept, seen, TN) + info_a
    shift = row_mm(off_a + row_mm(vec_b, spr_as), settle, NT)
    off = row_mm(shift, move_bs, NT) + off_b
    vec = row_mm(vec_b - row_mm(off_a, info_bs), kept) + vec_a
    return moved, info, spread, off, vec


def applies(state, seconds):
    settles = resolvents([(state[0], second[1]) for second in seconds])
    return [applied(state, *item) for item in zip(seconds, settles)]


def apply(state, second):
    return applies(state, [second])[0]


def applied(state, second, settle):
    spr_a, off_a = state
    move_b, info_b, spr_b, off_b, vec_b = second
    settle = split(settle)
    spr_as, move_bs = split(spr_a), split(move_b)
    narrowed = split(mm(settle, spr_as))
    spread = mm(mm(move_bs, narrowed), move_bs, NT) + spr_b
    shift = row_mm(off_a + row_mm(vec_b, spr_as), settle, NT)
    off = row_mm(shift, move_bs, NT) + off_b
    return spread, off


def fetch(sources, buffers, sems):
    copies = []
    for source, buffer in zip(sources, buffers):
        copies.append(pltpu.make_async_copy(source, buffer, sems.at[len(copies)]))
    for copy in copies:
        copy.start()
    for copy in copies:
        copy.wait()


def local_kernel(
    flag, prefixes, total, forward, observe, noise, measured, noise_state, mean, cov, begin, lead
):
    steps, n = forward.shape[0], forward.shape[1]

    @pl.when(flag[0] == 1)
    def _():
        ahead = split(forward[0])
        begin[0] = mm(mm(ahead, cov[...]), ahead, NT) + noise_state[...]
        begin[1] = jnp.zeros((n, n), F32)
        lead[...] = mm(wide(mean[...]), ahead, NT)

    @pl.when(flag[0] == 0)
    def _():
        begin[0] = noise_state[...]
        begin[1] = forward[0]
        lead[...] = jnp.zeros((8, n), F32)

    weights = [1.0 / noise[t : t + 1, :] for t in range(steps)]
    infos = [mm(jnp.transpose(observe[t]) * weights[t], observe[t]) for t in range(steps)]
    spreads = [begin[0] if t == 0 else noise_state[...] for t in range(steps)]
    settles = resolvents(list(zip(spreads, infos)))
    running = None
    for t in range(steps):
        vec_obs = row_mm(measured[t : t + 1, :] * weights[t], observe[t])
        settle, process = split(settles[t]), split(spreads[t])
        ahead = split(begin[1] if t == 0 else forward[t])
        moved = mm(settle, ahead)
        moveds = split(moved)
        spread = mm(settle, process)
        shift = row_mm(vec_obs, process)
        off = row_mm(shift + lead[0:1, :] if t == 0 else shift, settle, NT)
        info = mm(moveds, split(mm(infos[t], ahead)), TN)
        element = (moved, info, spread, off, row_mm(vec_obs, moveds))
        running = element if running is None else combine(running, element)
        write(prefixes.at[t], running)
    write(total, running)


def total_kernel(flag, total, mine, other):
    @pl.when(flag[0] == 1)
    def _():
        write(total, combine(read(other), read(mine)))

    @pl.when(flag[0] == 0)
    def _():
        write(total, combine(read(mine), read(other)))


def entering_kernel(flag, entering, other, before=None):
    n = other.shape[1]

    @pl.when(flag[0] == 1)
    def _():
        if before is None:
            entering[...] = other[...]
        else:
            write(entering, combine(read(other), read(before)))

    @pl.when(flag[0] == 0)
    def _():
        if before is None:
            zero, row = jnp.zeros((n, n), F32), jnp.zeros((1, n), F32)
            write(entering, (eye(n), zero, zero, row, row))
        else:
            entering[...] = before[...]


def state_kernel(flag, state, mine, other):
    n = mine.shape[1]

    def go(first, second):
        write_compact(state, apply(read_state(first, n + n // 2), read(second)))

    @pl.when(flag[0] == 1)
    def _():
        go(other, mine)

    @pl.when(flag[0] == 0)
    def _():
        go(mine, other)


def compose_kernel(flag, composed, other, before, prefixes):
    steps = range(prefixes.shape[0])

    @pl.when(flag[0] == 1)
    def _():
        write(before, combine(read(other), read(before)))

    made = combines([read(before)] * len(steps), [read(prefixes.at[t]) for t in steps])
    for t in steps:
        write(composed.at[t], made[t])


def final_kernel(flag, means, covs, other, prefixes):
    n = prefixes.shape[2]
    steps = range(prefixes.shape[0])

    @pl.when(flag[0] == 1)
    def _():
        made = applies(read_compact(other), [read(prefixes.at[t]) for t in steps])
        for t in steps:
            covs[t] = made[t][0]
            means[t : t + 1, :] = made[t][1]

    @pl.when(flag[0] == 0)
    def _():
        for t in steps:
            cov, mean = read_state(prefixes.at[t], n + n // 2)
            covs[t] = cov
            means[t : t + 1, :] = mean


def call(kernel, args, outs, scratch=()):
    flag, operands = args[0], args[1:]
    vmem = pl.BlockSpec(memory_space=pltpu.VMEM)

    def body(flag, *refs):
        count, made = len(operands), len(outs)
        sources, results = refs[:count], refs[count : count + made]
        buffers, sems = refs[count + made : 2 * count + made], refs[2 * count + made]
        fetch(sources, buffers, sems)
        kernel(flag, *results, *buffers, *refs[2 * count + made + 1 :])

    return pl.pallas_call(
        body,
        out_shape=[jax.ShapeDtypeStruct(s, F32) for s in outs],
        in_specs=[pl.BlockSpec(memory_space=pltpu.SMEM)]
        + [pl.BlockSpec(memory_space=pltpu.HBM)] * len(operands),
        out_specs=[vmem] * len(outs),
        scratch_shapes=[pltpu.VMEM(a.shape, F32) for a in operands]
        + [pltpu.SemaphoreType.DMA((len(operands),))]
        + [pltpu.VMEM(shape, F32) for shape in scratch],
        name=kernel.__name__,
        cost_estimate=pl.CostEstimate(
            flops=3000000000, bytes_accessed=4000000, transcendentals=0
        ),
        compiler_params=pltpu.CompilerParams(
            vmem_limit_bytes=WHOLE if kernel is local_kernel else LIMIT
        ),
    )(*args)


def on_device(transition, observe, noise_obs, measured, noise_state, prior_mean, prior_cov):
    steps, n = transition.shape[0], transition.shape[1]
    rows = packed_rows(n)
    axes = ("grp", "dev")
    grp, dev = lax.axis_index("grp"), lax.axis_index("dev")
    groups, devs = lax.axis_size("grp"), lax.axis_size("dev")
    places = [(g, d) for g in range(groups) for d in range(devs)]

    def flags(value):
        return jnp.asarray(value, jnp.int32)[None]

    def send(array, route):
        pairs = []
        for g, d in places:
            to = route(g, d)
            if to is not None:
                pairs.append((g * devs + d, to[0] * devs + to[1]))
        return lax.ppermute(array, axes, pairs)

    first = jnp.logical_and(grp == 0, dev == 0)
    prefixes, total = call(
        local_kernel,
        (
            flags(first),
            transition,
            observe,
            noise_obs,
            measured,
            noise_state,
            prior_mean[None],
            prior_cov,
        ),
        [(steps, rows, n), (rows, n)],
        [(2, n, n), (8, n)],
    )
    rounds = [("dev", 1 << b) for b in range(devs.bit_length() - 1)]
    rounds += [("grp", 1 << b) for b in range(groups.bit_length() - 1)]
    before = None
    for count, (axis, gap) in enumerate(rounds):
        upper = flags(((dev if axis == "dev" else grp) // gap) % 2)

        def across(g, d):
            return (g, d ^ gap) if axis == "dev" else (g ^ gap, d)

        if count < len(rounds) - 1:
            other = send(total, across)
            if before is not None:
                other, before = lax.optimization_barrier((other, before))
            if count < len(rounds) - 2:
                (total,) = call(total_kernel, (upper, total, other), [(rows, n)])
                (before,) = call(
                    entering_kernel,
                    (upper, other) + (() if before is None else (before,)),
                    [(rows, n)],
                )
            else:
                (state,) = call(state_kernel, (upper, total, other), [(compact_rows(n), n)])
                (composed,) = call(
                    compose_kernel, (upper, other, before, prefixes), [(steps, rows, n)]
                )
        else:
            received = send(state, lambda g, d: None if g & gap else across(g, d))
            means, covs = call(
                final_kernel, (upper, received, composed), [(steps, n), (steps, n, n)]
            )
    return means, covs


def solution(mesh):
    both = ("grp", "dev")
    return jax.shard_map(
        on_device,
        mesh=mesh,
        in_specs=(P(both, None, None), P(both, None, None), P(both, None), P(both, None), P(), P(), P()),
        out_specs=(P(both, None), P(both, None, None)),
        check_vma=False,
    )
```
